32 devices in a mesh: prompt: 4 (over x, core), branch: 8 (over z, y).
Axes of the slice: x: 2, y: 2, z: 4, core: 2. Of those that a mesh axis runs over, the one named last changes fastest.
Arguments:
- query: bfloat16 [32, 512, 2048], P(('prompt', 'branch')), may hold values from -6 to 6
- branch_kv: bfloat16 [32, 512, 2, 1024], P(('prompt', 'branch'))
- prefix_kv: bfloat16 [128, 2, 1024], P(('prompt', 'branch'))
- cotangent: bfloat16 [32, 512, 2048], P(('prompt', 'branch')), may hold values from -48 to 48
- subtree_end: int32 [32, 512], P(('prompt', 'branch')), may hold values from 1 to 512, as said below
- lengths: int32 [32], P(('prompt', 'branch')), may hold values from 1 to 512, as said below
Outputs:
- attended: bfloat16 [32, 512, 2048], P(('prompt', 'branch'))
- query_grad: bfloat16 [32, 512, 2048], P(('prompt', 'branch'))
- branch_kv_grad: bfloat16 [32, 512, 2, 1024], P(('prompt', 'branch'))
- prefix_kv_grad: bfloat16 [128, 2, 1024], P(('prompt', 'branch'))
The draws below stay inside these ranges and needn't reach their ends.
Inputs may be any that keep to these rules, and one draw needn't show every extreme that they name: The positions of each branch are in depth-first order of a token tree rooted at position 0; subtree_end[b, t] is one past the last position of the subtree under t, so it exceeds t, and the root's value is 512. Positions from lengths[b] on are padding; some branch has all 512 positions live.
All inputs are finite; a program needn't handle non-finite values.
Results may differ from the reference program's by a relative error of at most 0.0071.
Values may be sent and summed in bfloat16 or wider, within the bound.
A program may use at most 128 MiB of HBM per device.

```python
import math
import jax
import jax.numpy as jnp
from jax import lax

QUERY_HEADS = 16
KEY_VALUE_HEADS = 8
HEAD_SIZE = 128
BRANCH_LENGTH = 512
BRANCHES = 32
PROMPT_TOKENS = 128


def key_value_rows(key, lead, low, high):
    first, second, third = jax.random.split(key, 3)
    feature_width = KEY_VALUE_HEADS * HEAD_SIZE
    row_scale = jnp.exp(jax.random.uniform(first, lead + (1, 1), jnp.float32, math.log(low), math.log(high)))
    col_scale = jnp.exp(jax.random.uniform(second, lead + (1, feature_width), jnp.float32, math.log(0.5), math.log(2.0)))
    gauss = jax.random.normal(third, lead + (2, feature_width), jnp.float32)
    base = gauss
    key_scale = row_scale * col_scale
    scale = jnp.concatenate([key_scale, jnp.ones_like(key_scale)], axis=-2)
    return (base * scale).astype(jnp.bfloat16)


def draw_branch_kv(key, part):
    key = jax.random.fold_in(key, 13)
    return key_value_rows(key, (BRANCHES, BRANCH_LENGTH), 0.3, 3.0)


def draw_prefix_kv(key, part):
    key = jax.random.fold_in(key, 14)
    return key_value_rows(key, (PROMPT_TOKENS,), 0.3, 3.0)


def draw_subtree_end(key, part):
    key = jax.random.fold_in(key, 12)
    first, second = jax.random.split(key)
    forks = jax.random.randint(first, (BRANCHES, BRANCH_LENGTH), 0, 24)
    picks = jax.random.randint(second, (BRANCHES, BRANCH_LENGTH), 0, 1 << 20)

    def advance(depth, item):
        fork, pick = item
        following = jnp.where(fork == 0, 1 + pick % jnp.maximum(depth, 1), depth + 1).astype(jnp.int32)
        return (following, following)

    def one_tree(items):
        fork, pick = items
        _, depths = lax.scan(advance, jnp.zeros((), jnp.int32), (fork[1:], pick[1:]))
        depths = jnp.concatenate([jnp.zeros((1,), jnp.int32), depths])
        places = jnp.arange(BRANCH_LENGTH, dtype=jnp.int32)
        later = (places[None, :] > places[:, None]) & (depths[None, :] <= depths[:, None])
        return jnp.min(jnp.where(later, places[None, :], BRANCH_LENGTH), axis=1).astype(jnp.int32)
    return lax.map(one_tree, (forks, picks))


def draw_lengths(key, part):
    key = jax.random.fold_in(key, 11)
    first, second = jax.random.split(key)
    drawn = jax.random.randint(first, (BRANCHES,), 1, BRANCH_LENGTH + 1)
    longest = jax.random.randint(second, (), 0, BRANCHES)
    return jnp.where(jnp.arange(BRANCHES) == longest, BRANCH_LENGTH, drawn).astype(jnp.int32)


def level_of(own_key, shape, pieces, low, high):
    def one(axis_at, blocks):
        steps = jax.random.uniform(jax.random.fold_in(jax.random.fold_in(own_key, 6), axis_at), (blocks,), jnp.float32, low / len(pieces), high / len(pieces))
        return jnp.repeat(jnp.exp(steps), shape[axis_at] // blocks).reshape((-1,) + (1,) * (len(shape) - axis_at - 1))

    level = one(*pieces[0])
    for cut in pieces[1:]:
        level = level * one(*cut)
    return level


def normal_values(key, shape, scale, reach, cuts=(), kind=jnp.bfloat16):
    values = scale * jax.random.normal(key, shape, jnp.float32)
    if cuts:
        values = values * level_of(key, shape, cuts, -0.22, 0.18)
    return jnp.clip(values, -reach, reach).astype(kind)


def setup_inputs(seed: int = 0) -> dict:
    seeds = jax.random.split(jax.random.key(seed), 7)
    return {
        "query": normal_values(seeds[0], (BRANCHES, BRANCH_LENGTH, QUERY_HEADS * HEAD_SIZE), 1.0, 6.0, ((0, 32),)),
        "branch_kv": draw_branch_kv(jax.random.fold_in(seeds[6], 71), 0),
        "prefix_kv": draw_prefix_kv(jax.random.fold_in(seeds[6], 71), 0),
        "cotangent": normal_values(seeds[3], (BRANCHES, BRANCH_LENGTH, QUERY_HEADS * HEAD_SIZE), 8.0, 48.0, ((0, 32),)),
        "subtree_end": draw_subtree_end(jax.random.fold_in(seeds[6], 71), 0),
        "lengths": draw_lengths(jax.random.fold_in(seeds[6], 71), 0),
    }


SOFTCAP = 50.0
QUERY_SCALE = 144.0 ** -0.5


def bf16_round(values):
    return lax.optimization_barrier(values.astype(jnp.bfloat16)).astype(jnp.float32)


def group_terms(queries, grads_in, keys, values, visible):
    high = lax.Precision.HIGHEST
    raw = jnp.einsum("qrd,nd->rqn", queries, keys, precision=high)
    capped = SOFTCAP * jnp.tanh(raw * QUERY_SCALE / SOFTCAP)
    weights = jnp.where(visible[None], jnp.exp(capped), 0.0)
    total = jnp.sum(weights, axis=-1)
    probs = weights / total[..., None]
    probs_b = bf16_round(probs)
    context = jnp.einsum("rqn,nd->qrd", probs_b, values, precision=high)
    grad_prob = jnp.einsum("qrd,nd->rqn", grads_in, values, precision=high)
    delta = jnp.transpose(jnp.sum(grads_in * context, axis=-1))
    score_grad = bf16_round(probs * (grad_prob - delta[..., None]) * (1.0 - (capped / SOFTCAP) ** 2) * QUERY_SCALE)
    dquery = jnp.einsum("rqn,nd->qrd", score_grad, keys, precision=high)
    dkey = jnp.einsum("rqn,qrd->nd", score_grad, queries, precision=high)
    dvalue = jnp.einsum("rqn,qrd->nd", probs_b, grads_in, precision=high)
    return context, dquery, jnp.stack([dkey, dvalue], axis=1)


def reference(query, branch_kv, prefix_kv, cotangent, subtree_end, lengths):
    query_group_ratio = QUERY_HEADS // KEY_VALUE_HEADS

    def one_branch(items):
        rows_q, rows_kv, rows_cot, ends, length = items
        positions = jnp.arange(BRANCH_LENGTH, dtype=jnp.int32)
        live = positions < length
        keys_all = jnp.concatenate([prefix_kv, rows_kv], axis=0).astype(jnp.float32)
        tree = (positions[None, :] <= positions[:, None]) & (positions[:, None] < ends[None, :])
        visible = jnp.concatenate([jnp.ones((BRANCH_LENGTH, PROMPT_TOKENS), dtype=bool), tree], axis=1)
        queries = rows_q.astype(jnp.float32).reshape(BRANCH_LENGTH, QUERY_HEADS, HEAD_SIZE)
        grads_in = jnp.where(live[:, None], rows_cot, jnp.zeros_like(rows_cot)).astype(jnp.float32).reshape(BRANCH_LENGTH, QUERY_HEADS, HEAD_SIZE)

        def heads_per_group(index):
            q_g = lax.dynamic_slice_in_dim(queries, index * query_group_ratio, query_group_ratio, 1)
            g_g = lax.dynamic_slice_in_dim(grads_in, index * query_group_ratio, query_group_ratio, 1)
            kv_g = lax.dynamic_slice_in_dim(keys_all, index * HEAD_SIZE, HEAD_SIZE, 2)
            return group_terms(q_g, g_g, kv_g[:, 0], kv_g[:, 1], visible)

        context_outputs, query_gradients, key_value_gradients = lax.map(heads_per_group, jnp.arange(KEY_VALUE_HEADS, dtype=jnp.int32))
        context = jnp.transpose(context_outputs, (1, 0, 2, 3)).reshape(BRANCH_LENGTH, QUERY_HEADS * HEAD_SIZE)
        attended = jnp.where(live[:, None], context, 0.0).astype(jnp.bfloat16)
        dquery = jnp.transpose(query_gradients, (1, 0, 2, 3)).reshape(BRANCH_LENGTH, QUERY_HEADS * HEAD_SIZE).astype(jnp.bfloat16)
        key_value_gradient = jnp.transpose(key_value_gradients, (1, 2, 0, 3)).reshape(PROMPT_TOKENS + BRANCH_LENGTH, 2, KEY_VALUE_HEADS * HEAD_SIZE)
        return attended, dquery, key_value_gradient[PROMPT_TOKENS:].astype(jnp.bfloat16), key_value_gradient[:PROMPT_TOKENS]

    attended, query_grad, branch_kv_grad, prefix_parts = lax.map(
        one_branch, (query, branch_kv, cotangent, subtree_end, lengths))
    prefix_kv_grad = jnp.sum(prefix_parts, axis=0).astype(jnp.bfloat16)
    return attended, query_grad, branch_kv_grad, prefix_kv_grad
```

```python
import functools

import jax
import jax.numpy as jnp
from jax import lax
from jax.experimental import pallas as pl
from jax.experimental.pallas import tpu as pltpu
from jax.sharding import PartitionSpec as P

QUERY_HEADS = 16
KEY_VALUE_HEADS = 8
HEAD_SIZE = 128
RATIO = QUERY_HEADS // KEY_VALUE_HEADS

softcap = 50.0
query_scale = 144.0 ** (-0.5)
MESH = pl.DeviceIdType.MESH
QB = 256
KC = 128


def nt(a, b):
    return lax.dot_general(a, b, (((1,), (1,)), ((), ())), preferred_element_type=jnp.float32)


def nn(a, b):
    return jnp.dot(a, b, preferred_element_type=jnp.float32)


def greet(peers):
    barrier = pltpu.get_barrier_semaphore()
    for peer in peers:
        pl.semaphore_signal(barrier, inc=1, device_id=peer, device_id_type=MESH)
    pl.semaphore_wait(barrier, len(peers))


def exchange_peers(n_p, n_b):
    p, b = lax.axis_index("prompt"), lax.axis_index("branch")
    ring = [(p, lax.rem(b + k, n_b)) for k in range(1, n_b)]
    pairs = []
    step = 1
    while step < n_p:
        low = lax.rem(lax.div(p, step), 2)
        pairs.append((p + step - 2 * step * low, b))
        step *= 2
    return p, b, ring, pairs


def gather_kernel(n_p, n_b, src, out, send_b, recv_b, send_p, recv_p, own_sem):
    rows = src.shape[0]
    p, b, ring, pairs = exchange_peers(n_p, n_b)
    greet(ring + pairs)
    mine = out.at[pl.ds((p * n_b + b) * rows, rows)]
    local = pltpu.make_async_copy(src, mine, own_sem)
    local.start()
    copies = []
    for k, peer in enumerate(ring):
        copy = pltpu.make_async_remote_copy(
            src_ref=src, dst_ref=mine, send_sem=send_b.at[k], recv_sem=recv_b.at[k],
            device_id=peer, device_id_type=MESH)
        copy.start()
        copies.append(copy)
    local.wait()
    for copy in copies:
        copy.wait()
    step = 1
    for k, peer in enumerate(pairs):
        first = lax.div(p, step) * step
        part = out.at[pl.ds(first * n_b * rows, step * n_b * rows)]
        copy = pltpu.make_async_remote_copy(
            src_ref=part, dst_ref=part, send_sem=send_p.at[k], recv_sem=recv_p.at[k],
            device_id=peer, device_id_type=MESH)
        copy.start()
        copy.wait()
        step *= 2


def gather_prefix(n_p, n_b, prefix_kv):
    rows = prefix_kv.shape[0]
    n_k = max(n_p.bit_length() - 1, 1)
    return pl.pallas_call(
        functools.partial(gather_kernel, n_p, n_b),
        out_shape=jax.ShapeDtypeStruct((rows * n_p * n_b,) + prefix_kv.shape[1:], prefix_kv.dtype),
        in_specs=[pl.BlockSpec(memory_space=pl.ANY)],
        out_specs=pl.BlockSpec(memory_space=pl.ANY),
        scratch_shapes=[
            pltpu.SemaphoreType.DMA((n_b,)),
            pltpu.SemaphoreType.DMA((n_b,)),
            pltpu.SemaphoreType.DMA((n_k,)),
            pltpu.SemaphoreType.DMA((n_k,)),
            pltpu.SemaphoreType.DMA,
        ],
        compiler_params=pltpu.CompilerParams(collective_id=0, has_side_effects=True),
        name="gather_prefix",
    )(prefix_kv)


def scatter_kernel(n_p, n_b, term, out, work, land_p, land_b, send_p, recv_p, send_b, recv_b):
    p, b, ring, pairs = exchange_peers(n_p, n_b)
    greet(ring + pairs)
    src = term
    step = n_p // 2
    first = 0
    at = 0
    for k in range(len(pairs)):
        pass
    width = n_p
    parts = list(range(n_p))
    step = 1
    level = 0
    while step < n_p:
        peer = pairs[level]
        bit = lax.rem(lax.div(p, step), 2)
        half = n_p // (2 * step)
        copies = []
        low = lax.rem(p, step)
        for i in range(half):
            theirs = low + (1 - bit) * step + i * 2 * step
            source = src.at[pl.ds(theirs * n_b, n_b)]
            copy = pltpu.make_async_remote_copy(
                src_ref=source, dst_ref=land_p.at[pl.ds((at + i) * n_b, n_b)],
                send_sem=send_p.at[at + i], recv_sem=recv_p.at[at + i],
                device_id=peer, device_id_type=MESH)
            copy.start()
            copies.append(copy)
        for copy in copies:
            copy.wait()
        for i in range(half):
            ours = low + bit * step + i * 2 * step
            own = src[pl.ds(ours * n_b, n_b)].astype(jnp.float32)
            got = land_p[pl.ds((at + i) * n_b, n_b)].astype(jnp.float32)
            work[pl.ds(ours * n_b, n_b)] = (own + got).astype(work.dtype)
        src = work
        at += half
        step *= 2
        level += 1
    copies = []
    for k, (_, other) in enumerate(ring):
        copy = pltpu.make_async_remote_copy(
            src_ref=src.at[p * n_b + other], dst_ref=land_b.at[k],
            send_sem=send_b.at[k], recv_sem=recv_b.at[k],
            device_id=(p, other), device_id_type=MESH)
        copy.start()
        copies.append(copy)
    total = src[p * n_b + b].astype(jnp.float32)
    for copy in copies:
        copy.wait()
    for k in range(len(ring)):
        total += land_b[k].astype(jnp.float32)
    out[...] = total.astype(out.dtype)


def scatter_prefix(n_p, n_b, term):
    blocks, high, wide = term.shape
    n_k = max(n_p - 1, 1)
    return pl.pallas_call(
        functools.partial(scatter_kernel, n_p, n_b),
        out_shape=jax.ShapeDtypeStruct((high, wide), jnp.bfloat16),
        in_specs=[pl.BlockSpec(memory_space=pltpu.VMEM)],
        out_specs=pl.BlockSpec(memory_space=pltpu.VMEM),
        scratch_shapes=[
            pltpu.VMEM((blocks, high, wide), term.dtype),
            pltpu.VMEM((n_k * n_b, high, wide), term.dtype),
            pltpu.VMEM((n_b, high, wide), term.dtype),
            pltpu.SemaphoreType.DMA((n_k,)),
            pltpu.SemaphoreType.DMA((n_k,)),
            pltpu.SemaphoreType.DMA((n_b,)),
            pltpu.SemaphoreType.DMA((n_b,)),
        ],
        compiler_params=pltpu.CompilerParams(collective_id=1, has_side_effects=True,
                                             vmem_limit_bytes=24 * 1024 * 1024),
        name="scatter_prefix",
    )(term)


def attention_kernel(lens, ends, q_ref, g_ref, kv_ref, pkv_ref, att, qg, kvg, pg,
                     mask, k_all, v_all, kt, vt, p_s, t_s, ds_s):
    rows = q_ref.shape[0]
    prefix = pkv_ref.shape[1]
    length = lens[0]

    @pl.when(pl.program_id(0) == 0)
    def _():
        for r in range(0, rows, KC):
            span = jnp.broadcast_to(ends[:, r:r + KC].astype(jnp.float32), (KC, KC))
            stop = jnp.transpose(span)[:, :1]
            t = lax.broadcasted_iota(jnp.int32, (KC, rows), 0) + r
            i = lax.broadcasted_iota(jnp.int32, (KC, rows), 1)
            seen = (t <= i) & (i.astype(jnp.float32) < stop)
            mask[r:r + KC, :] = jnp.where(seen, 1.0, 0.0)

    k_all[:prefix] = pkv_ref[0]
    k_all[prefix:] = kv_ref[0]
    v_all[:prefix] = pkv_ref[1]
    v_all[prefix:] = kv_ref[1]
    kt[...] = jnp.transpose(k_all[...])
    vt[...] = jnp.transpose(v_all[...])

    dk = [None] * ((prefix + rows) // KC)
    dv = [None] * ((prefix + rows) // KC)
    for h in range(RATIO):
        cols = slice(h * HEAD_SIZE, (h + 1) * HEAD_SIZE)
        for j in range(rows // QB):
            spot = slice(j * QB, (j + 1) * QB)
            n = prefix + (j + 1) * QB
            chunks = n // KC
            live = lax.broadcasted_iota(jnp.int32, (QB, HEAD_SIZE), 0) + j * QB < length
            q = q_ref[spot, cols]
            g = jnp.where(live, g_ref[spot, cols], jnp.zeros((), jnp.bfloat16))
            total = jnp.zeros((1, QB), jnp.float32)
            for c in range(chunks):
                at = slice(c * KC, (c + 1) * KC)
                t = jnp.tanh(nt(k_all[at], q) * (query_scale / softcap))
                w = jnp.exp(softcap * t)
                if c * KC >= prefix:
                    w = w * mask[c * KC - prefix:(c + 1) * KC - prefix, spot]
                total += jnp.sum(w, axis=0, keepdims=True)
                p_s[at] = w
                t_s[at] = t
            inverse = 1.0 / total
            probs = []
            for c in range(chunks):
                at = slice(c * KC, (c + 1) * KC)
                p = p_s[at] * inverse
                p_s[at] = p
                probs.append(p.astype(jnp.bfloat16))
            probs = jnp.concatenate(probs, axis=0)
            context = nn(vt[:, :n], probs)
            delta = jnp.sum(jnp.transpose(g).astype(jnp.float32) * context, axis=0, keepdims=True)
            att[spot, cols] = jnp.where(
                live, jnp.transpose(context.astype(jnp.bfloat16)), jnp.zeros((), jnp.bfloat16))
            for c in range(chunks):
                at = slice(c * KC, (c + 1) * KC)
                t = t_s[at]
                score = p_s[at] * (nt(v_all[at], g) - delta) * (1.0 - t * t)
                ds_s[at] = score.astype(jnp.bfloat16)
            scores = ds_s[:n]
            dq = nn(kt[:, :n], scores) * query_scale
            qg[spot, cols] = jnp.transpose(dq.astype(jnp.bfloat16))
            for c in range(chunks):
                at = slice(c * KC, (c + 1) * KC)
                one = nn(scores[at], q)
                two = nn(probs[at], g)
                dk[c] = one if dk[c] is None else dk[c] + one
                dv[c] = two if dv[c] is None else dv[c] + two
    for c in range(len(dk)):
        if c * KC < prefix:
            pg[0, c * KC:(c + 1) * KC] = dk[c] * query_scale
            pg[1, c * KC:(c + 1) * KC] = dv[c]
        else:
            at = slice(c * KC - prefix, (c + 1) * KC - prefix)
            kvg[0, at] = (dk[c] * query_scale).astype(jnp.bfloat16)
            kvg[1, at] = dv[c].astype(jnp.bfloat16)


def attention(lengths, ends, query, cotangent, kv, pkv):
    rows, wide = query.shape
    prefix = pkv.shape[1]
    every = prefix + rows
    pair = RATIO * HEAD_SIZE
    return pl.pallas_call(
        attention_kernel,
        grid=(KEY_VALUE_HEADS,),
        in_specs=[
            pl.BlockSpec(memory_space=pltpu.SMEM),
            pl.BlockSpec((1, rows), lambda i: (0, 0)),
            pl.BlockSpec((rows, pair), lambda i: (0, i)),
            pl.BlockSpec((rows, pair), lambda i: (0, i)),
            pl.BlockSpec((2, rows, HEAD_SIZE), lambda i: (0, 0, i)),
            pl.BlockSpec((2, prefix, HEAD_SIZE), lambda i: (0, 0, i)),
        ],
        out_specs=[
            pl.BlockSpec((rows, pair), lambda i: (0, i)),
            pl.BlockSpec((rows, pair), lambda i: (0, i)),
            pl.BlockSpec((2, rows, HEAD_SIZE), lambda i: (0, 0, i)),
            pl.BlockSpec((2, prefix, HEAD_SIZE), lambda i: (0, 0, i)),
        ],
        out_shape=[
            jax.ShapeDtypeStruct((rows, wide), jnp.bfloat16),
            jax.ShapeDtypeStruct((rows, wide), jnp.bfloat16),
            jax.ShapeDtypeStruct(kv.shape, jnp.bfloat16),
            jax.ShapeDtypeStruct(pkv.shape, jnp.float32),
        ],
        scratch_shapes=[
            pltpu.VMEM((rows, rows), jnp.float32),
            pltpu.VMEM((every, HEAD_SIZE), jnp.bfloat16),
            pltpu.VMEM((every, HEAD_SIZE), jnp.bfloat16),
            pltpu.VMEM((HEAD_SIZE, every), jnp.bfloat16),
            pltpu.VMEM((HEAD_SIZE, every), jnp.bfloat16),
            pltpu.VMEM((every, QB), jnp.float32),
            pltpu.VMEM((every, QB), jnp.float32),
            pltpu.VMEM((every, QB), jnp.bfloat16),
        ],
        compiler_params=pltpu.CompilerParams(vmem_limit_bytes=40 * 1024 * 1024),
        name="attention",
    )(lengths, ends, query, cotangent, kv, pkv)


def body(n_p, n_b, query, branch_kv, prefix_kv, cotangent, subtree_end, lengths):
    own = prefix_kv.shape
    gathered = gather_prefix(n_p, n_b, prefix_kv)
    pkv = jnp.transpose(gathered, (1, 0, 2))
    kv = jnp.transpose(branch_kv[0], (1, 0, 2))
    att, qg, kvg, pg = attention(lengths, subtree_end, query[0], cotangent[0], kv, pkv)
    term = jnp.transpose(pg, (1, 0, 2)).astype(jnp.bfloat16)
    size = own[0] * own[1] * own[2]
    mine = scatter_prefix(n_p, n_b, term.reshape(n_p * n_b, 16, size // 16))
    return att[None], qg[None], jnp.transpose(kvg, (1, 0, 2))[None], mine.reshape(own)


def solution(mesh):
    both = ("prompt", "branch")
    in_specs = (
        P(both, None, None),
        P(both, None, None, None),
        P(both, None, None),
        P(both, None, None),
        P(both, None),
        P(both),
    )
    out_specs = (
        P(both, None, None),
        P(both, None, None),
        P(both, None, None, None),
        P(both, None, None),
    )
    part = functools.partial(body, mesh.shape["prompt"], mesh.shape["branch"])
    return jax.shard_map(part, mesh=mesh, in_specs=in_specs, out_specs=out_specs, check_vma=False)
```

```python
import functools

import jax
import jax.numpy as jnp
from jax import lax
from jax.experimental import pallas as pl
from jax.experimental.pallas import tpu as pltpu
from jax.sharding import PartitionSpec as P

QUERY_HEADS = 16
KEY_VALUE_HEADS = 8
HEAD_SIZE = 128
RATIO = QUERY_HEADS // KEY_VALUE_HEADS

softcap = 50.0
query_scale = 144.0 ** (-0.5)
MESH = pl.DeviceIdType.MESH
QB = 256
KC = 128


def nt(a, b):
    return lax.dot_general(a, b, (((1,), (1,)), ((), ())), preferred_element_type=jnp.float32)


def nn(a, b):
    return jnp.dot(a, b, preferred_element_type=jnp.float32)


def attention_kernel(n_p, n_b, pair_count, lens, ends, q_ref, g_ref, kv_ref, own_ref, att, qg, kvg, pg,
                     mask, pick, lay, w_s, t_s, k_all, v_all, kt, vt, ds_s,
                     ahead, terms, carry, land, ag_send, ag_recv, rs_send, rs_recv):
    rows = q_ref.shape[0]
    prefix = pick.shape[1] // 2
    devices = n_p * n_b
    length = lens[0]
    step = pl.program_id(0)
    groups = KEY_VALUE_HEADS
    group = lax.rem(step, groups)
    blocks = rows // QB
    p, b = lax.axis_index("prompt"), lax.axis_index("branch")
    me = p * n_b + b

    def peer(k):
        return (lax.rem(p + k // n_b, n_p), lax.rem(b + lax.rem(k, n_b), n_b))

    def gather_copy(part, k):
        return pltpu.make_async_remote_copy(
            src_ref=own_ref.at[part], dst_ref=ahead.at[part, me],
            send_sem=ag_send.at[part, k], recv_sem=ag_recv.at[part, k],
            device_id=peer(k), device_id_type=MESH)

    def return_copy(part, k):
        to_p, to_b = peer(k)
        return pltpu.make_async_remote_copy(
            src_ref=terms.at[part, to_p * n_b + to_b], dst_ref=land.at[part, k],
            send_sem=rs_send.at[part, k], recv_sem=rs_recv.at[part, k],
            device_id=(to_p, to_b), device_id_type=MESH)

    def each(act):
        def turn(k, _):
            act(k)
            return 0
        lax.fori_loop(1, devices, turn, 0)

    @pl.when(step == 0)
    def _():
        barrier = pltpu.get_barrier_semaphore()
        each(lambda k: pl.semaphore_signal(barrier, inc=1, device_id=peer(k), device_id_type=MESH))
        for r in range(0, rows, KC):
            span = jnp.broadcast_to(ends[:, r:r + KC].astype(jnp.float32), (KC, KC))
            stop = jnp.transpose(span)[:, :1]
            t = lax.broadcasted_iota(jnp.int32, (KC, rows), 0) + r
            i = lax.broadcasted_iota(jnp.int32, (KC, rows), 1)
            seen = (t <= i) & (i.astype(jnp.float32) < stop)
            mask[r:r + KC, :] = jnp.where(seen, 1.0, 0.0)

    @pl.when(step == 2)
    def _():
        pl.semaphore_wait(pltpu.get_barrier_semaphore(), devices - 1)
        for part in range(pair_count):
            each(lambda k: gather_copy(part, k).start())
            ahead[part, me] = own_ref[part]

    @pl.when(step == 1)
    def _():
        per = prefix // devices
        half = 2 * per
        wide = pick.shape[2]
        for parity in range(2):
            row = lax.broadcasted_iota(jnp.int32, (2 * prefix, wide), 0)
            col = lax.broadcasted_iota(jnp.int32, (2 * prefix, wide), 1)
            kv = row // prefix
            at = row - kv * prefix
            want = (at // per) * (2 * half) + parity * half + kv * per + at % per
            pick[parity] = jnp.where(want == col, 1.0, 0.0).astype(jnp.bfloat16)
            row = lax.broadcasted_iota(jnp.int32, (wide, 2 * prefix), 0)
            col = lax.broadcasted_iota(jnp.int32, (wide, 2 * prefix), 1)
            kv = col // prefix
            at = col - kv * prefix
            want = (at // per) * (2 * half) + parity * half + kv * per + at % per
            lay[parity] = jnp.where(want == row, 1.0, 0.0).astype(jnp.bfloat16)

    units = []
    base = 0
    for h in range(RATIO):
        for j in range(blocks):
            units.append((h, j, base))
            base += (j + 1) * QB

    @pl.when(step < groups)
    def _():
        for h, j, base in units:
            cols = slice(h * HEAD_SIZE, (h + 1) * HEAD_SIZE)
            spot = slice(j * QB, (j + 1) * QB)
            q = q_ref[spot, cols]
            for c in range((j + 1) * QB // KC):
                at = slice(c * KC, (c + 1) * KC)
                t = jnp.tanh(nt(kv_ref[0, at], q) * (query_scale / softcap))
                w = jnp.exp(softcap * t) * mask[at, spot]
                w_s[group, base + c * KC:base + (c + 1) * KC] = w
                t_s[group, base + c * KC:base + (c + 1) * KC] = t

    @pl.when((step >= groups) & (lax.rem(step, 2) == 0))
    def _():
        each(lambda k: gather_copy(group // 2, k).wait_recv())

    @pl.when(step >= groups)
    def _():
        part = group // 2
        parity = lax.rem(group, 2)
        arrived = ahead[part].reshape(pick.shape[2], HEAD_SIZE)
        prompt_rows = nn(pick[parity], arrived).astype(jnp.bfloat16)
        k_all[:prefix] = prompt_rows[:prefix]
        k_all[prefix:] = kv_ref[0]
        v_all[:prefix] = prompt_rows[prefix:]
        v_all[prefix:] = kv_ref[1]
        kt[...] = jnp.transpose(k_all[...])
        vt[...] = jnp.transpose(v_all[...])

        dk = [None] * ((prefix + rows) // KC)
        dv = [None] * ((prefix + rows) // KC)
        for h, j, base in units:
            cols = slice(h * HEAD_SIZE, (h + 1) * HEAD_SIZE)
            spot = slice(j * QB, (j + 1) * QB)
            n = prefix + (j + 1) * QB
            chunks = n // KC
            live = lax.broadcasted_iota(jnp.int32, (QB, HEAD_SIZE), 0) + j * QB < length
            q = q_ref[spot, cols]
            g = jnp.where(live, g_ref[spot, cols], jnp.zeros((), jnp.bfloat16))
            total = jnp.zeros((1, QB), jnp.float32)
            first = {}
            for c in range(chunks):
                if c * KC < prefix:
                    t = jnp.tanh(nt(k_all[c * KC:(c + 1) * KC], q) * (query_scale / softcap))
                    w = jnp.exp(softcap * t)
                    first[c] = (w, t)
                else:
                    w = w_s[group, base + c * KC - prefix:base + (c + 1) * KC - prefix]
                total += jnp.sum(w, axis=0, keepdims=True)
            inverse = 1.0 / total

            def weights(c):
                if c in first:
                    return first[c]
                at = slice(base + c * KC - prefix, base + (c + 1) * KC - prefix)
                return w_s[group, at], t_s[group, at]

            probs = []
            for c in range(chunks):
                probs.append((weights(c)[0] * inverse).astype(jnp.bfloat16))
            probs = jnp.concatenate(probs, axis=0)
            context = nn(vt[:, :n], probs)
            delta = jnp.sum(jnp.transpose(g).astype(jnp.float32) * context, axis=0, keepdims=True)
            att[spot, cols] = jnp.where(
                live, jnp.transpose(context.astype(jnp.bfloat16)), jnp.zeros((), jnp.bfloat16))
            for c in range(chunks):
                at = slice(c * KC, (c + 1) * KC)
                w, t = weights(c)
                score = (w * inverse) * (nt(v_all[at], g) - delta) * (1.0 - t * t)
                ds_s[at] = score.astype(jnp.bfloat16)
            scores = ds_s[:n]
            dq = nn(kt[:, :n], scores) * query_scale
            qg[spot, cols] = jnp.transpose(dq.astype(jnp.bfloat16))
            for c in range(chunks):
                at = slice(c * KC, (c + 1) * KC)
                one = nn(scores[at], q)
                two = nn(probs[at], g)
                dk[c] = one if dk[c] is None else dk[c] + one
                dv[c] = two if dv[c] is None else dv[c] + two
        sums = []
        for c in range(len(dk)):
            if c * KC < prefix:
                sums.append((dk[c], dv[c]))
            else:
                at = slice(c * KC - prefix, (c + 1) * KC - prefix)
                kvg[0, at] = (dk[c] * query_scale).astype(jnp.bfloat16)
                kvg[1, at] = dv[c].astype(jnp.bfloat16)
        stack = jnp.concatenate([s[0] * query_scale for s in sums] + [s[1] for s in sums], axis=0)
        placed = nn(lay[parity], stack.astype(jnp.bfloat16))

        @pl.when(parity == 0)
        def _():
            carry[...] = placed

        @pl.when(parity == 1)
        def _():
            terms[part] = (carry[...] + placed).astype(jnp.bfloat16).reshape(terms.shape[1:])
            each(lambda k: return_copy(part, k).start())

    @pl.when(step == 2 * groups - 1)
    def _():
        for part in range(pair_count):
            each(lambda k: gather_copy(part, k).wait_send())
            total = terms[part, me].astype(jnp.float32)

            def turn(k, total):
                return_copy(part, k).wait()
                return total + land[part, k].astype(jnp.float32)

            total = lax.fori_loop(1, devices, turn, total)
            pg[part] = total.astype(jnp.bfloat16)


def attention(n_p, n_b, lengths, ends, query, cotangent, kv, own):
    rows, wide = query.shape
    devices = n_p * n_b
    pair_count, high, _ = own.shape
    prefix = devices * (high // 4)
    every = prefix + rows
    pair = RATIO * HEAD_SIZE
    groups = KEY_VALUE_HEADS
    blocks = rows // QB
    stored = RATIO * QB * blocks * (blocks + 1) // 2
    late = lambda i: (0, (i // groups) * (i % groups))
    late3 = lambda i: (0, 0, (i // groups) * (i % groups))
    bf16, f32 = jnp.bfloat16, jnp.float32
    return pl.pallas_call(
        functools.partial(attention_kernel, n_p, n_b, pair_count),
        grid=(2 * groups,),
        in_specs=[
            pl.BlockSpec(memory_space=pltpu.SMEM),
            pl.BlockSpec((1, rows), lambda i: (0, 0)),
            pl.BlockSpec((rows, pair), lambda i: (0, i % groups)),
            pl.BlockSpec((rows, pair), late),
            pl.BlockSpec((2, rows, HEAD_SIZE), lambda i: (0, 0, i % groups)),
            pl.BlockSpec(memory_space=pltpu.VMEM),
        ],
        out_specs=[
            pl.BlockSpec((rows, pair), late),
            pl.BlockSpec((rows, pair), late),
            pl.BlockSpec((2, rows, HEAD_SIZE), late3),
            pl.BlockSpec((pair_count, high, HEAD_SIZE), lambda i: (0, 0, 0)),
        ],
        out_shape=[
            jax.ShapeDtypeStruct((rows, wide), bf16),
            jax.ShapeDtypeStruct((rows, wide), bf16),
            jax.ShapeDtypeStruct(kv.shape, bf16),
            jax.ShapeDtypeStruct(own.shape, bf16),
        ],
        scratch_shapes=[
            pltpu.VMEM((rows, rows), f32),
            pltpu.VMEM((2, 2 * prefix, devices * high), bf16),
            pltpu.VMEM((2, devices * high, 2 * prefix), bf16),
            pltpu.VMEM((groups, stored, QB), f32),
            pltpu.VMEM((groups, stored, QB), f32),
            pltpu.VMEM((every, HEAD_SIZE), bf16),
            pltpu.VMEM((every, HEAD_SIZE), bf16),
            pltpu.VMEM((HEAD_SIZE, every), bf16),
            pltpu.VMEM((HEAD_SIZE, every), bf16),
            pltpu.VMEM((every, QB), bf16),
            pltpu.VMEM((pair_count, devices, high, HEAD_SIZE), bf16),
            pltpu.VMEM((pair_count, devices, high, HEAD_SIZE), bf16),
            pltpu.VMEM((devices * high, HEAD_SIZE), f32),
            pltpu.VMEM((pair_count, devices, high, HEAD_SIZE), bf16),
            pltpu.SemaphoreType.DMA((pair_count, devices)),
            pltpu.SemaphoreType.DMA((pair_count, devices)),
            pltpu.SemaphoreType.DMA((pair_count, devices)),
            pltpu.SemaphoreType.DMA((pair_count, devices)),
        ],
        compiler_params=pltpu.CompilerParams(
            collective_id=0, has_side_effects=True, vmem_limit_bytes=58 * 1024 * 1024),
        name="attention",
    )(lengths, ends, query, cotangent, kv, own)


def body(n_p, n_b, query, branch_kv, prefix_kv, cotangent, subtree_end, lengths):
    per = prefix_kv.shape[0]
    pairs = KEY_VALUE_HEADS // 2
    own = jnp.transpose(prefix_kv.reshape(per, 2, pairs, 2, HEAD_SIZE), (2, 3, 1, 0, 4))
    own = own.reshape(pairs, 4 * per, HEAD_SIZE)
    kv = jnp.transpose(branch_kv[0], (1, 0, 2))
    att, qg, kvg, pg = attention(n_p, n_b, lengths, subtree_end, query[0], cotangent[0], kv, own)
    mine = jnp.transpose(pg.reshape(pairs, 2, 2, per, HEAD_SIZE), (3, 2, 0, 1, 4))
    return att[None], qg[None], jnp.transpose(kvg, (1, 0, 2))[None], mine.reshape(prefix_kv.shape)


def solution(mesh):
    both = ("prompt", "branch")
    in_specs = (
        P(both, None, None),
        P(both, None, None, None),
        P(both, None, None),
        P(both, None, None),
        P(both, None),
        P(both),
    )
    out_specs = (
        P(both, None, None),
        P(both, None, None),
        P(both, None, None, None),
        P(both, None, None),
    )
    part = functools.partial(body, mesh.shape["prompt"], mesh.shape["branch"])
    return jax.shard_map(part, mesh=mesh, in_specs=in_specs, out_specs=out_specs, check_vma=False)
```

```python
import functools

import jax
import jax.numpy as jnp
from jax import lax
from jax.experimental import pallas as pl
from jax.experimental.pallas import tpu as pltpu
from jax.sharding import PartitionSpec as P

QUERY_HEADS = 16
KEY_VALUE_HEADS = 8
HEAD_SIZE = 128
RATIO = QUERY_HEADS // KEY_VALUE_HEADS

softcap = 50.0
query_scale = 144.0 ** (-0.5)
MESH = pl.DeviceIdType.MESH
QB = 256
KC = 128


def nt(a, b):
    return lax.dot_general(a, b, (((1,), (1,)), ((), ())), preferred_element_type=jnp.float32)


def nn(a, b):
    return jnp.dot(a, b, preferred_element_type=jnp.float32)


def attention_kernel(n_p, n_b, pair_count, lens, ends, q_ref, g_ref, kv_ref, own_ref, att, qg, kvg, pg,
                     mask, pick, lay, w_s, t_s, d_s, k_s, v_s, kt_s, vt_s,
                     ahead, terms, carry, land, ag_send, ag_recv, rs_send, rs_recv):
    rows = q_ref.shape[0]
    devices = n_p * n_b
    high = own_ref.shape[1]
    prefix = devices * high // 4
    some = pick.shape[1] // 2
    wide = pick.shape[2]
    length = lens[0]
    step = pl.program_id(0)
    groups = KEY_VALUE_HEADS
    group = lax.rem(step, groups)
    blocks = rows // QB
    p, b = lax.axis_index("prompt"), lax.axis_index("branch")
    me = p * n_b + b

    def peer(k):
        return (lax.rem(p + k // n_b, n_p), lax.rem(b + k % n_b, n_b))

    def gather_copy(part, k):
        return pltpu.make_async_remote_copy(
            src_ref=own_ref.at[part], dst_ref=ahead.at[part, me],
            send_sem=ag_send.at[part], recv_sem=ag_recv.at[part],
            device_id=peer(k), device_id_type=MESH)

    def return_copy(part, k):
        to_p, to_b = peer(k)
        return pltpu.make_async_remote_copy(
            src_ref=terms.at[part, to_p * n_b + to_b], dst_ref=land.at[part, k],
            send_sem=rs_send.at[part], recv_sem=rs_recv.at[part],
            device_id=(to_p, to_b), device_id_type=MESH)

    def each(act):
        for k in range(1, devices):
            act(k)

    def settle(buffer, sem):
        span = buffer.at[pl.ds(0, devices - 1)]
        pltpu.make_async_copy(span, span, sem).wait()

    @pl.when(step == 0)
    def _():
        barrier = pltpu.get_barrier_semaphore()
        each(lambda k: pl.semaphore_signal(barrier, inc=1, device_id=peer(k), device_id_type=MESH))
        for r in range(0, rows, KC):
            span = jnp.broadcast_to(ends[:, r:r + KC].astype(jnp.float32), (KC, KC))
            stop = jnp.transpose(span)[:, :1]
            t = lax.broadcasted_iota(jnp.int32, (KC, rows), 0) + r
            i = lax.broadcasted_iota(jnp.int32, (KC, rows), 1)
            seen = (t <= i) & (i.astype(jnp.float32) < stop)
            mask[r:r + KC, :] = jnp.where(seen, 1.0, 0.0)

    def gather_start(part):
        each(lambda k: gather_copy(part, k).start())
        ahead[part, me] = own_ref[part]

    @pl.when(step == 4)
    def _():
        pl.semaphore_wait(pltpu.get_barrier_semaphore(), devices - 1)

    for part in range(pair_count):
        @pl.when(step == 4 + 2 * part)
        def _():
            gather_start(part)

    @pl.when(step == 1)
    def _():
        per = high // 4

        def place(shape, dim):
            line = lax.broadcasted_iota(jnp.int32, shape, dim)
            kv = line // some
            at = line - kv * some
            return (at // per) * (4 * per) + kv * per + at % per

        down = place((2 * some, 1), 0)
        over = place((1, 2 * some), 1)
        col = lax.broadcasted_iota(jnp.int32, (2 * some, wide), 1)
        row = lax.broadcasted_iota(jnp.int32, (wide, 2 * some), 0)
        for parity in range(2):
            shift = parity * 2 * per
            pick[parity] = jnp.where(down + shift == col, 1.0, 0.0).astype(jnp.bfloat16)
            lay[parity] = jnp.where(over + shift == row, 1.0, 0.0).astype(jnp.bfloat16)

    units = []
    base = 0
    for h in range(RATIO):
        for j in range(blocks):
            units.append((h, j, base))
            base += (j + 1) * QB

    def live_rows(j):
        return lax.broadcasted_iota(jnp.int32, (QB, HEAD_SIZE), 0) + j * QB < length

    def masked(j, spot, cols):
        return jnp.where(live_rows(j), g_ref[spot, cols], jnp.zeros((), jnp.bfloat16))

    @pl.when(step < groups)
    def _():
        keys = kv_ref[:, 0, :]
        values = kv_ref[:, 1, :]
        k_s[group] = keys
        v_s[group] = values
        kt_s[group] = jnp.transpose(keys)
        vt_s[group] = jnp.transpose(values)
        for h, j, base in units:
            cols = slice(h * HEAD_SIZE, (h + 1) * HEAD_SIZE)
            spot = slice(j * QB, (j + 1) * QB)
            q = q_ref[spot, cols]
            g = masked(j, spot, cols)
            for c in range((j + 1) * QB // KC):
                at = slice(c * KC, (c + 1) * KC)
                to = slice(base + c * KC, base + (c + 1) * KC)
                t = jnp.tanh(nt(keys[at], q) * (query_scale / softcap))
                w_s[group, to] = jnp.exp(softcap * t) * mask[at, spot]
                t_s[group, to] = t
                d_s[group, to] = nt(values[at], g)

    @pl.when((step >= groups) & (lax.rem(step, 2) == 0))
    def _():
        settle(ahead.at[group // 2], ag_recv.at[group // 2])

    @pl.when(step >= groups)
    def _():
        part = group // 2
        parity = lax.rem(group, 2)
        key_parts, value_parts = [], []
        for one in range(prefix // some):
            arrived = ahead[part, one * (wide // high):(one + 1) * (wide // high)].reshape(wide, HEAD_SIZE)
            lines = nn(pick[parity], arrived).astype(jnp.bfloat16)
            key_parts.append(lines[:some])
            value_parts.append(lines[some:])
        prompt_keys = jnp.concatenate(key_parts, axis=0)
        prompt_values = jnp.concatenate(value_parts, axis=0)
        prompt_kt = jnp.transpose(prompt_keys)
        prompt_vt = jnp.transpose(prompt_values)

        dk = [None] * ((prefix + rows) // KC)
        dv = [None] * ((prefix + rows) // KC)
        for h, j, base in units:
            cols = slice(h * HEAD_SIZE, (h + 1) * HEAD_SIZE)
            spot = slice(j * QB, (j + 1) * QB)
            tree = (j + 1) * QB
            chunks = (prefix + tree) // KC
            q = q_ref[spot, cols]
            g = masked(j, spot, cols)
            total = jnp.zeros((1, QB), jnp.float32)
            first = {}
            for c in range(chunks):
                if c * KC < prefix:
                    at = slice(c * KC, (c + 1) * KC)
                    t = jnp.tanh(nt(prompt_keys[at], q) * (query_scale / softcap))
                    w = jnp.exp(softcap * t)
                    first[c] = (w, t, nt(prompt_values[at], g))
                else:
                    w = w_s[group, base + c * KC - prefix:base + (c + 1) * KC - prefix]
                total += jnp.sum(w, axis=0, keepdims=True)
            inverse = 1.0 / total

            def weights(c):
                if c in first:
                    return first[c]
                at = slice(base + c * KC - prefix, base + (c + 1) * KC - prefix)
                return w_s[group, at], t_s[group, at], d_s[group, at]

            near = prefix // KC
            probs = [(weights(c)[0] * inverse).astype(jnp.bfloat16) for c in range(chunks)]
            context = nn(prompt_vt, jnp.concatenate(probs[:near], axis=0))
            context += nn(vt_s[group, :, :tree], jnp.concatenate(probs[near:], axis=0))
            delta = jnp.sum(jnp.transpose(g).astype(jnp.float32) * context, axis=0, keepdims=True)
            att[spot, cols] = jnp.where(
                live_rows(j), jnp.transpose(context.astype(jnp.bfloat16)), jnp.zeros((), jnp.bfloat16))
            scores = []
            for c in range(chunks):
                w, t, d = weights(c)
                scores.append(((w * inverse) * (d - delta) * (1.0 - t * t)).astype(jnp.bfloat16))
            dq = nn(prompt_kt, jnp.concatenate(scores[:near], axis=0))
            dq += nn(kt_s[group, :, :tree], jnp.concatenate(scores[near:], axis=0))
            qg[spot, cols] = jnp.transpose((dq * query_scale).astype(jnp.bfloat16))
            for c in range(chunks):
                one = nn(scores[c], q)
                two = nn(probs[c], g)
                dk[c] = one if dk[c] is None else dk[c] + one
                dv[c] = two if dv[c] is None else dv[c] + two
        sums = []
        for c in range(len(dk)):
            if c * KC < prefix:
                sums.append((dk[c], dv[c]))
            else:
                at = slice(c * KC - prefix, (c + 1) * KC - prefix)
                kvg[0, at] = (dk[c] * query_scale).astype(jnp.bfloat16)
                kvg[1, at] = dv[c].astype(jnp.bfloat16)
        all_k = jnp.concatenate([one[0] for one in sums], axis=0) * query_scale
        all_v = jnp.concatenate([one[1] for one in sums], axis=0)
        placed = []
        for one in range(prefix // some):
            at = slice(one * some, (one + 1) * some)
            stack = jnp.concatenate([all_k[at], all_v[at]], axis=0)
            placed.append(nn(lay[parity], stack.astype(jnp.bfloat16)))
        placed = jnp.concatenate(placed, axis=0)

        @pl.when(parity == 0)
        def _():
            carry[...] = placed

        @pl.when(parity == 1)
        def _():
            terms[part] = (carry[...] + placed).astype(jnp.bfloat16).reshape(terms.shape[1:])
            each(lambda k: return_copy(part, k).start())

    @pl.when(step == 2 * groups - 1)
    def _():
        for part in range(pair_count):
            settle(ahead.at[part], ag_send.at[part])
            settle(terms.at[part], rs_send.at[part])
            settle(land.at[part], rs_recv.at[part])
            total = terms[part, me].astype(jnp.float32)
            for k in range(1, devices):
                total += land[part, k].astype(jnp.float32)
            pg[part] = total.astype(jnp.bfloat16)


def attention(n_p, n_b, lengths, ends, query, cotangent, kv, own):
    rows, wide = query.shape
    devices = n_p * n_b
    pair_count, high, _ = own.shape
    prefix = devices * (high // 4)
    pair = RATIO * HEAD_SIZE
    groups = KEY_VALUE_HEADS
    blocks = rows // QB
    stored = RATIO * QB * blocks * (blocks + 1) // 2
    late = lambda i: (0, (i // groups) * (i % groups))
    late3 = lambda i: (0, 0, (i // groups) * (i % groups))
    early3 = lambda i: (0, 0, (1 - i // groups) * (i % groups) + (i // groups) * (groups - 1))
    some = prefix // max(devices // 32, 1)
    wide_pair = 4 * some
    bf16, f32 = jnp.bfloat16, jnp.float32
    return pl.pallas_call(
        functools.partial(attention_kernel, n_p, n_b, pair_count),
        grid=(2 * groups,),
        in_specs=[
            pl.BlockSpec(memory_space=pltpu.SMEM),
            pl.BlockSpec((1, rows), lambda i: (0, 0)),
            pl.BlockSpec((rows, pair), lambda i: (0, i % groups)),
            pl.BlockSpec((rows, pair), lambda i: (0, i % groups)),
            pl.BlockSpec((rows, 2, HEAD_SIZE), early3),
            pl.BlockSpec(memory_space=pltpu.VMEM),
        ],
        out_specs=[
            pl.BlockSpec((rows, pair), late),
            pl.BlockSpec((rows, pair), late),
            pl.BlockSpec((2, rows, HEAD_SIZE), late3),
            pl.BlockSpec((pair_count, high, HEAD_SIZE), lambda i: (0, 0, 0)),
        ],
        out_shape=[
            jax.ShapeDtypeStruct((rows, wide), bf16),
            jax.ShapeDtypeStruct((rows, wide), bf16),
            jax.ShapeDtypeStruct((2, rows, kv.shape[2]), bf16),
            jax.ShapeDtypeStruct(own.shape, bf16),
        ],
        scratch_shapes=[
            pltpu.VMEM((rows, rows), f32),
            pltpu.VMEM((2, 2 * some, wide_pair), bf16),
            pltpu.VMEM((2, wide_pair, 2 * some), bf16),
            pltpu.VMEM((groups, stored, QB), f32),
            pltpu.VMEM((groups, stored, QB), f32),
            pltpu.VMEM((groups, stored, QB), f32),
            pltpu.VMEM((groups, rows, HEAD_SIZE), bf16),
            pltpu.VMEM((groups, rows, HEAD_SIZE), bf16),
            pltpu.VMEM((groups, HEAD_SIZE, rows), bf16),
            pltpu.VMEM((groups, HEAD_SIZE, rows), bf16),
            pltpu.VMEM((pair_count, devices, high, HEAD_SIZE), bf16),
            pltpu.VMEM((pair_count, devices, high, HEAD_SIZE), bf16),
            pltpu.VMEM((devices * high, HEAD_SIZE), f32),
            pltpu.VMEM((pair_count, devices, high, HEAD_SIZE), bf16),
            pltpu.SemaphoreType.DMA((pair_count,)),
            pltpu.SemaphoreType.DMA((pair_count,)),
            pltpu.SemaphoreType.DMA((pair_count,)),
            pltpu.SemaphoreType.DMA((pair_count,)),
        ],
        compiler_params=pltpu.CompilerParams(
            collective_id=0, has_side_effects=True, vmem_limit_bytes=58 * 1024 * 1024),
        name="attention",
    )(lengths, ends, query, cotangent, kv, own)


def body(n_p, n_b, query, branch_kv, prefix_kv, cotangent, subtree_end, lengths):
    per = prefix_kv.shape[0]
    pairs = KEY_VALUE_HEADS // 2
    own = jnp.transpose(prefix_kv.reshape(per, 2, pairs, 2, HEAD_SIZE), (2, 3, 1, 0, 4))
    own = own.reshape(pairs, 4 * per, HEAD_SIZE)
    kv = branch_kv[0]
    att, qg, kvg, pg = attention(n_p, n_b, lengths, subtree_end, query[0], cotangent[0], kv, own)
    mine = jnp.transpose(pg.reshape(pairs, 2, 2, per, HEAD_SIZE), (3, 2, 0, 1, 4))
    return att[None], qg[None], jnp.transpose(kvg, (1, 0, 2))[None], mine.reshape(prefix_kv.shape)


def solution(mesh):
    both = ("prompt", "branch")
    in_specs = (
        P(both, None, None),
        P(both, None, None, None),
        P(both, None, None),
        P(both, None, None),
        P(both, None),
        P(both),
    )
    out_specs = (
        P(both, None, None),
        P(both, None, None),
        P(both, None, None, None),
        P(both, None, None),
    )
    part = functools.partial(body, mesh.shape["prompt"], mesh.shape["branch"])
    return jax.shard_map(part, mesh=mesh, in_specs=in_specs, out_specs=out_specs, check_vma=False)
```

```python
import functools

import jax
import jax.numpy as jnp
from jax import lax
from jax.experimental import pallas as pl
from jax.experimental.pallas import tpu as pltpu
from jax.sharding import PartitionSpec as P

QUERY_HEADS = 16
KEY_VALUE_HEADS = 8
HEAD_SIZE = 128
RATIO = QUERY_HEADS // KEY_VALUE_HEADS

softcap = 50.0
query_scale = 144.0 ** (-0.5)
MESH = pl.DeviceIdType.MESH
QB = 256
KC = 128


def nt(a, b):
    return lax.dot_general(a, b, (((1,), (1,)), ((), ())), preferred_element_type=jnp.float32)


def nn(a, b):
    return jnp.dot(a, b, preferred_element_type=jnp.float32)


def attention_kernel(n_p, n_b, pair_count, lens, ends, q_ref, g_ref, kv_ref, own_ref, att, qg, kvg, pg,
                     mask, pick, lay, w_s, t_s, d_s, k_s, v_s, kt_s, vt_s,
                     ahead, terms, carry, land, ag_send, ag_recv, rs_send, rs_recv):
    rows = q_ref.shape[0]
    devices = n_p * n_b
    high = own_ref.shape[1]
    prefix = devices * high // 4
    some = pick.shape[1] // 2
    wide = pick.shape[2]
    length = lens[0]
    step = pl.program_id(0)
    groups = KEY_VALUE_HEADS
    group = lax.rem(step, groups)
    blocks = rows // QB
    p, b = lax.axis_index("prompt"), lax.axis_index("branch")
    me = p * n_b + b

    def peer(k):
        return (lax.rem(p + k // n_b, n_p), lax.rem(b + k % n_b, n_b))

    def gather_copy(part, k):
        return pltpu.make_async_remote_copy(
            src_ref=own_ref.at[pl.ds(2 * part, 2)], dst_ref=ahead.at[part, me],
            send_sem=ag_send.at[part], recv_sem=ag_recv.at[part],
            device_id=peer(k), device_id_type=MESH)

    def return_copy(part, k):
        to_p, to_b = peer(k)
        return pltpu.make_async_remote_copy(
            src_ref=terms.at[part, to_p * n_b + to_b], dst_ref=land.at[part, k],
            send_sem=rs_send.at[part], recv_sem=rs_recv.at[part],
            device_id=(to_p, to_b), device_id_type=MESH)

    def each(act):
        for k in range(1, devices):
            act(k)

    def settle(buffer, sem):
        span = buffer.at[pl.ds(0, devices - 1)]
        pltpu.make_async_copy(span, span, sem).wait()

    @pl.when(step == 0)
    def _():
        barrier = pltpu.get_barrier_semaphore()
        each(lambda k: pl.semaphore_signal(barrier, inc=1, device_id=peer(k), device_id_type=MESH))
        for r in range(0, rows, KC):
            span = jnp.broadcast_to(ends[:, r:r + KC].astype(jnp.float32), (KC, KC))
            stop = jnp.transpose(span)[:, :1]
            t = lax.broadcasted_iota(jnp.int32, (KC, rows), 0) + r
            i = lax.broadcasted_iota(jnp.int32, (KC, rows), 1)
            seen = (t <= i) & (i.astype(jnp.float32) < stop)
            mask[r:r + KC, :] = jnp.where(seen, 1.0, 0.0)

    def gather_start(part):
        each(lambda k: gather_copy(part, k).start())
        ahead[part, me] = own_ref[2 * part:2 * part + 2]

    @pl.when(step == 4)
    def _():
        pl.semaphore_wait(pltpu.get_barrier_semaphore(), devices - 1)

    for part in range(pair_count // 2):
        @pl.when(step == 4 + 4 * part)
        def _():
            gather_start(part)

    @pl.when(step == 1)
    def _():
        per = high // 4

        def place(shape, dim):
            line = lax.broadcasted_iota(jnp.int32, shape, dim)
            kv = line // some
            at = line - kv * some
            return (at // per) * (4 * per) + kv * per + at % per

        down = place((2 * some, 1), 0)
        over = place((1, 2 * some), 1)
        col = lax.broadcasted_iota(jnp.int32, (2 * some, wide), 1)
        row = lax.broadcasted_iota(jnp.int32, (wide, 2 * some), 0)
        for parity in range(2):
            shift = parity * 2 * per
            pick[parity] = jnp.where(down + shift == col, 1.0, 0.0).astype(jnp.bfloat16)
            lay[parity] = jnp.where(over + shift == row, 1.0, 0.0).astype(jnp.bfloat16)

    units = []
    base = 0
    for h in range(RATIO):
        for j in range(blocks):
            units.append((h, j, base))
            base += (j + 1) * QB

    def live_rows(j):
        return lax.broadcasted_iota(jnp.int32, (QB, HEAD_SIZE), 0) + j * QB < length

    def masked(j, spot, cols):
        return jnp.where(live_rows(j), g_ref[spot, cols], jnp.zeros((), jnp.bfloat16))

    @pl.when(step < groups)
    def _():
        keys = kv_ref[:, 0, :]
        values = kv_ref[:, 1, :]
        k_s[group] = keys
        v_s[group] = values
        kt_s[group] = jnp.transpose(keys)
        vt_s[group] = jnp.transpose(values)
        for h, j, base in units:
            cols = slice(h * HEAD_SIZE, (h + 1) * HEAD_SIZE)
            spot = slice(j * QB, (j + 1) * QB)
            q = q_ref[spot, cols]
            g = masked(j, spot, cols)
            for c in range((j + 1) * QB // KC):
                at = slice(c * KC, (c + 1) * KC)
                to = slice(base + c * KC, base + (c + 1) * KC)
                t = jnp.tanh(nt(keys[at], q) * (query_scale / softcap))
                w_s[group, to] = jnp.exp(softcap * t) * mask[at, spot]
                t_s[group, to] = t
                d_s[group, to] = nt(values[at], g)

    @pl.when((step >= groups) & (lax.rem(step, 4) == 0))
    def _():
        settle(ahead.at[group // 4], ag_recv.at[group // 4])

    @pl.when(step >= groups)
    def _():
        part = group // 2
        parity = lax.rem(group, 2)
        key_parts, value_parts = [], []
        for one in range(prefix // some):
            arrived = ahead[part // 2, one * (wide // high):(one + 1) * (wide // high), lax.rem(part, 2)].reshape(wide, HEAD_SIZE)
            lines = nn(pick[parity], arrived).astype(jnp.bfloat16)
            key_parts.append(lines[:some])
            value_parts.append(lines[some:])
        prompt_keys = jnp.concatenate(key_parts, axis=0)
        prompt_values = jnp.concatenate(value_parts, axis=0)
        prompt_kt = jnp.transpose(prompt_keys)
        prompt_vt = jnp.transpose(prompt_values)

        dk = [None] * ((prefix + rows) // KC)
        dv = [None] * ((prefix + rows) // KC)
        for h, j, base in units:
            cols = slice(h * HEAD_SIZE, (h + 1) * HEAD_SIZE)
            spot = slice(j * QB, (j + 1) * QB)
            tree = (j + 1) * QB
            chunks = (prefix + tree) // KC
            q = q_ref[spot, cols]
            g = masked(j, spot, cols)
            total = jnp.zeros((1, QB), jnp.float32)
            first = {}
            for c in range(chunks):
                if c * KC < prefix:
                    at = slice(c * KC, (c + 1) * KC)
                    t = jnp.tanh(nt(prompt_keys[at], q) * (query_scale / softcap))
                    w = jnp.exp(softcap * t)
                    first[c] = (w, t, nt(prompt_values[at], g))
                else:
                    w = w_s[group, base + c * KC - prefix:base + (c + 1) * KC - prefix]
                total += jnp.sum(w, axis=0, keepdims=True)
            inverse = 1.0 / total

            def weights(c):
                if c in first:
                    return first[c]
                at = slice(base + c * KC - prefix, base + (c + 1) * KC - prefix)
                return w_s[group, at], t_s[group, at], d_s[group, at]

            near = prefix // KC
            probs = [(weights(c)[0] * inverse).astype(jnp.bfloat16) for c in range(chunks)]
            context = nn(prompt_vt, jnp.concatenate(probs[:near], axis=0))
            context += nn(vt_s[group, :, :tree], jnp.concatenate(probs[near:], axis=0))
            delta = jnp.sum(jnp.transpose(g).astype(jnp.float32) * context, axis=0, keepdims=True)
            att[spot, cols] = jnp.where(
                live_rows(j), jnp.transpose(context.astype(jnp.bfloat16)), jnp.zeros((), jnp.bfloat16))
            scores = []
            for c in range(chunks):
                w, t, d = weights(c)
                scores.append(((w * inverse) * (d - delta) * (1.0 - t * t)).astype(jnp.bfloat16))
            dq = nn(prompt_kt, jnp.concatenate(scores[:near], axis=0))
            dq += nn(kt_s[group, :, :tree], jnp.concatenate(scores[near:], axis=0))
            qg[spot, cols] = jnp.transpose((dq * query_scale).astype(jnp.bfloat16))
            for c in range(chunks):
                one = nn(scores[c], q)
                two = nn(probs[c], g)
                dk[c] = one if dk[c] is None else dk[c] + one
                dv[c] = two if dv[c] is None else dv[c] + two
        sums = []
        for c in range(len(dk)):
            if c * KC < prefix:
                sums.append((dk[c], dv[c]))
            else:
                at = slice(c * KC - prefix, (c + 1) * KC - prefix)
                kvg[0, at] = (dk[c] * query_scale).astype(jnp.bfloat16)
                kvg[1, at] = dv[c].astype(jnp.bfloat16)
        all_k = jnp.concatenate([one[0] for one in sums], axis=0) * query_scale
        all_v = jnp.concatenate([one[1] for one in sums], axis=0)
        placed = []
        for one in range(prefix // some):
            at = slice(one * some, (one + 1) * some)
            stack = jnp.concatenate([all_k[at], all_v[at]], axis=0)
            placed.append(nn(lay[parity], stack.astype(jnp.bfloat16)))
        placed = jnp.concatenate(placed, axis=0)

        @pl.when(parity == 0)
        def _():
            carry[...] = placed

        @pl.when(parity == 1)
        def _():
            terms[part] = (carry[...] + placed).astype(jnp.bfloat16).reshape(terms.shape[1:])
            each(lambda k: return_copy(part, k).start())

    @pl.when(step == 2 * groups - 1)
    def _():
        for part in range(pair_count):
            if part % 2 == 0:
                settle(ahead.at[part // 2], ag_send.at[part // 2])
            settle(terms.at[part], rs_send.at[part])
            settle(land.at[part], rs_recv.at[part])
            total = terms[part, me].astype(jnp.float32)
            for k in range(1, devices):
                total += land[part, k].astype(jnp.float32)
            pg[part] = total.astype(jnp.bfloat16)


def attention(n_p, n_b, lengths, ends, query, cotangent, kv, own):
    rows, wide = query.shape
    devices = n_p * n_b
    pair_count, high, _ = own.shape
    prefix = devices * (high // 4)
    pair = RATIO * HEAD_SIZE
    groups = KEY_VALUE_HEADS
    blocks = rows // QB
    stored = RATIO * QB * blocks * (blocks + 1) // 2
    late = lambda i: (0, (i // groups) * (i % groups))
    late3 = lambda i: (0, 0, (i // groups) * (i % groups))
    early3 = lambda i: (0, 0, (1 - i // groups) * (i % groups) + (i // groups) * (groups - 1))
    some = prefix // max(devices // 32, 1)
    wide_pair = 4 * some
    bf16, f32 = jnp.bfloat16, jnp.float32
    return pl.pallas_call(
        functools.partial(attention_kernel, n_p, n_b, pair_count),
        grid=(2 * groups,),
        in_specs=[
            pl.BlockSpec(memory_space=pltpu.SMEM),
            pl.BlockSpec((1, rows), lambda i: (0, 0)),
            pl.BlockSpec((rows, pair), lambda i: (0, i % groups)),
            pl.BlockSpec((rows, pair), lambda i: (0, i % groups)),
            pl.BlockSpec((rows, 2, HEAD_SIZE), early3),
            pl.BlockSpec(memory_space=pltpu.VMEM),
        ],
        out_specs=[
            pl.BlockSpec((rows, pair), late),
            pl.BlockSpec((rows, pair), late),
            pl.BlockSpec((2, rows, HEAD_SIZE), late3),
            pl.BlockSpec((pair_count, high, HEAD_SIZE), lambda i: (0, 0, 0)),
        ],
        out_shape=[
            jax.ShapeDtypeStruct((rows, wide), bf16),
            jax.ShapeDtypeStruct((rows, wide), bf16),
            jax.ShapeDtypeStruct((2, rows, kv.shape[2]), bf16),
            jax.ShapeDtypeStruct(own.shape, bf16),
        ],
        scratch_shapes=[
            pltpu.VMEM((rows, rows), f32),
            pltpu.VMEM((2, 2 * some, wide_pair), bf16),
            pltpu.VMEM((2, wide_pair, 2 * some), bf16),
            pltpu.VMEM((groups, stored, QB), f32),
            pltpu.VMEM((groups, stored, QB), f32),
            pltpu.VMEM((groups, stored, QB), f32),
            pltpu.VMEM((groups, rows, HEAD_SIZE), bf16),
            pltpu.VMEM((groups, rows, HEAD_SIZE), bf16),
            pltpu.VMEM((groups, HEAD_SIZE, rows), bf16),
            pltpu.VMEM((groups, HEAD_SIZE, rows), bf16),
            pltpu.VMEM((pair_count // 2, devices, 2, high, HEAD_SIZE), bf16),
            pltpu.VMEM((pair_count, devices, high, HEAD_SIZE), bf16),
            pltpu.VMEM((devices * high, HEAD_SIZE), f32),
            pltpu.VMEM((pair_count, devices, high, HEAD_SIZE), bf16),
            pltpu.SemaphoreType.DMA((pair_count,)),
            pltpu.SemaphoreType.DMA((pair_count,)),
            pltpu.SemaphoreType.DMA((pair_count,)),
            pltpu.SemaphoreType.DMA((pair_count,)),
        ],
        compiler_params=pltpu.CompilerParams(
            collective_id=0, has_side_effects=True, vmem_limit_bytes=58 * 1024 * 1024),
        name="attention",
    )(lengths, ends, query, cotangent, kv, own)


def body(n_p, n_b, query, branch_kv, prefix_kv, cotangent, subtree_end, lengths):
    per = prefix_kv.shape[0]
    pairs = KEY_VALUE_HEADS // 2
    own = jnp.transpose(prefix_kv.reshape(per, 2, pairs, 2, HEAD_SIZE), (2, 3, 1, 0, 4))
    own = own.reshape(pairs, 4 * per, HEAD_SIZE)
    kv = branch_kv[0]
    att, qg, kvg, pg = attention(n_p, n_b, lengths, subtree_end, query[0], cotangent[0], kv, own)
    mine = jnp.transpose(pg.reshape(pairs, 2, 2, per, HEAD_SIZE), (3, 2, 0, 1, 4))
    return att[None], qg[None], jnp.transpose(kvg, (1, 0, 2))[None], mine.reshape(prefix_kv.shape)


def solution(mesh):
    both = ("prompt", "branch")
    in_specs = (
        P(both, None, None),
        P(both, None, None, None),
        P(both, None, None),
        P(both, None, None),
        P(both, None),
        P(both),
    )
    out_specs = (
        P(both, None, None),
        P(both, None, None),
        P(both, None, None, None),
        P(both, None, None),
    )
    part = functools.partial(body, mesh.shape["prompt"], mesh.shape["branch"])
    return jax.shard_map(part, mesh=mesh, in_specs=in_specs, out_specs=out_specs, check_vma=False)
```
